128 devices in a mesh: ha: 4 (over y_hi, core), wa: 32 (over y_lo, x, z).
Axes of the slice: x: 4, y: 4 (y_hi: 2, y_lo: 2; y = y_hi * 2 + y_lo), z: 4, core: 2. Of those that a mesh axis runs over, the one named last changes fastest.
Arguments:
- queries: bfloat16 [8, 32, 384, 1536], P('ha', 'wa'), may hold values from -8 to 8
- keys: bfloat16 [8, 32, 384, 1536], P('ha', 'wa'), may hold values from -8 to 8
- values: bfloat16 [8, 32, 384, 1536], P('ha', 'wa'), may hold values from -6 to 6
- selected: int32 [8, 32, 32], P('ha', 'wa'), may hold values from 0 to 767, as said below
- counts: int32 [8, 32], P('ha', 'wa'), may hold values from 16 to 32, as said below
Outputs:
- mixed: bfloat16 [8, 32, 384, 1536], P('ha', 'wa')
The draws below stay inside these ranges and needn't reach their ends.
Inputs may be any that keep to these rules, and one draw needn't show every extreme that they name: `selected`: an entry names a cube of the reading tile's band of 2 tile rows as in the reference program. Of the 64 entries of one device's tiles, live or not, at most 2 name cubes of any one column, and in every band one column is named by exactly 2 entries of every device of the band. Only the first counts entries of a tile's list are live; some tile has all 32 live.
All inputs are finite; a program needn't handle non-finite values.
Results may differ from the reference program's by a relative error of at most 0.0035.
Values may be sent and summed in bfloat16 or wider, within the bound.
No kernel may reach another device: no remote copies, remote signals or barrier semaphores. Data moves between devices by JAX's collectives and lax.ppermute only.
A program may use at most 256 MiB of HBM per device.

```python
import jax
import jax.numpy as jnp
from jax import lax

H = 12
HEAD = 128
TILE = 384
CUBE = 32
SEL = 32
TILE_ROWS = 2
HD = 1536
CUBES_TILE = 12
CUBES_DEV = 24
CAP = 2
TILES_H = 8
TILES_W = 32


def draw_queries(key, part):
    key = jax.random.fold_in(key, 11)
    shape_all = (TILES_H, TILES_W, TILE, HD)
    result = jnp.clip(1.5 * jax.random.normal(key, shape_all, jnp.float32), -8.0, 8.0)
    return result.astype(jnp.bfloat16)


def draw_keys(key, part):
    key = jax.random.fold_in(key, 13)
    shape_all = (TILES_H, TILES_W, TILE, HD)
    result = jnp.clip(1.5 * jax.random.normal(key, shape_all, jnp.float32), -8.0, 8.0)
    return result.astype(jnp.bfloat16)


def draw_selected(key, part):
    key = jax.random.fold_in(key, 23)
    first_key, second_key, third_key = jax.random.split(key, 3)
    bands = TILES_H // TILE_ROWS
    hot = jax.random.randint(first_key, (bands,), 0, TILES_W)
    perm_keys = jax.random.split(second_key, bands * TILES_W)
    perms = jax.vmap(lambda one_key: jax.random.permutation(one_key, TILES_W))(perm_keys)
    perms = perms.reshape(bands, TILES_W, TILES_W).astype(jnp.int32)
    leading = perms[..., 0:1]
    hot_cols = hot[:, None, None].astype(jnp.int32)
    perms = jnp.where(perms == hot_cols, leading, perms)
    perms = perms.at[..., 0].set(jnp.broadcast_to(hot[:, None], (bands, TILES_W)).astype(jnp.int32))
    slot_group = jnp.arange(TILE_ROWS * SEL, dtype=jnp.int32) // CAP
    owners = jnp.take(perms, slot_group, axis=2)
    local_ids = jax.random.randint(third_key, owners.shape, 0, CUBES_DEV).astype(jnp.int32)
    cube_ids = owners * CUBES_DEV + local_ids
    cube_ids = cube_ids.reshape(bands, TILES_W, TILE_ROWS, SEL)
    cube_ids = jnp.transpose(cube_ids, (0, 2, 1, 3)).reshape(TILES_H, TILES_W, SEL)
    return cube_ids.astype(jnp.int32)


def draw_counts(key, part):
    key = jax.random.fold_in(key, 37)
    first_key, second_key = jax.random.split(key)
    base = jax.random.randint(first_key, (TILES_H * TILES_W,), SEL // 2, SEL + 1).astype(jnp.int32)
    spot = jax.random.randint(second_key, (), 0, TILES_H * TILES_W)
    base = base.at[spot].set(SEL)
    return base.reshape(TILES_H, TILES_W).astype(jnp.int32)


def shard_levels(key, extent, cuts, least, high):
    def one(dim, blocks):
        draws = jax.random.uniform(jax.random.fold_in(jax.random.fold_in(key, 6), dim), (blocks,), jnp.float32, least / len(cuts), high / len(cuts))
        return jnp.repeat(jnp.exp(draws), extent[dim] // blocks).reshape((-1,) + (1,) * (len(extent) - dim - 1))

    loudness = one(*cuts[0])
    for cut in cuts[1:]:
        loudness = loudness * one(*cut)
    return loudness


def gaussian(key, dims, width, bound, pieces=(), kind=jnp.bfloat16):
    entries = jax.random.normal(key, dims, jnp.float32) * width
    if len(pieces) > 0:
        entries = shard_levels(key, dims, pieces, -0.22, 0.18) * entries
    return jnp.clip(entries, min=-bound, max=bound).astype(kind)


def setup_inputs(seed: int = 0) -> dict:
    key_of = jax.random.split(jax.random.key(seed), 6)
    return {
        "queries": draw_queries(jax.random.fold_in(key_of[5], 71), 0),
        "keys": draw_keys(jax.random.fold_in(key_of[5], 71), 0),
        "values": gaussian(key_of[2], (TILES_H, TILES_W, TILE, HD), 1.0, 6.0, ((0, 4), (1, 32))),
        "selected": draw_selected(jax.random.fold_in(key_of[5], 71), 0),
        "counts": draw_counts(jax.random.fold_in(key_of[5], 71), 0),
    }


def reference(queries, keys, values, selected, counts):
    tiles_h = queries.shape[0]
    tiles_w = queries.shape[1]
    padded_keys = jnp.pad(keys, ((1, 1), (1, 1), (0, 0), (0, 0)))
    padded_vals = jnp.pad(values, ((1, 1), (1, 1), (0, 0), (0, 0)))
    offsets = jnp.arange(3, dtype=jnp.int32) - 1
    score_scale = float(HEAD) ** -0.5

    def one_tile(index):
        tile_row = index // tiles_w
        tile_col = index % tiles_w
        zero = jnp.zeros((), jnp.int32)
        corner = (tile_row, tile_col, zero, zero)
        win_keys = lax.dynamic_slice(padded_keys, corner, (3, 3, TILE, HD)).reshape(9 * TILE, HD)
        win_vals = lax.dynamic_slice(padded_vals, corner, (3, 3, TILE, HD)).reshape(9 * TILE, HD)
        row_ok = (tile_row + offsets >= 0) & (tile_row + offsets < tiles_h)
        col_ok = (tile_col + offsets >= 0) & (tile_col + offsets < tiles_w)
        window_ok = jnp.repeat((row_ok[:, None] & col_ok[None, :]).reshape(9), TILE)
        cube_ids = selected[tile_row, tile_col].astype(jnp.int32)
        band_row = tile_row // TILE_ROWS
        owner_col = (cube_ids // CUBES_DEV).astype(jnp.int32)
        cube_idx = cube_ids % CUBES_DEV
        src_rows = (band_row * TILE_ROWS + cube_idx // CUBES_TILE).astype(jnp.int32)
        starts = ((cube_idx % CUBES_TILE) * CUBE).astype(jnp.int32)

        def take(table):
            def single(row_at, col_at, start_at):
                return lax.dynamic_slice(table, (row_at, col_at, start_at, zero), (1, 1, CUBE, HD)).reshape(CUBE, HD)
            return jax.vmap(single)(src_rows, owner_col, starts).reshape(SEL * CUBE, HD)

        live_slots = jnp.repeat(jnp.arange(SEL, dtype=jnp.int32) < counts[tile_row, tile_col], CUBE)
        all_keys = jnp.concatenate([win_keys, take(keys)], axis=0).astype(jnp.float32)
        all_vals = jnp.concatenate([win_vals, take(values)], axis=0).astype(jnp.float32)
        usable = jnp.concatenate([window_ok, live_slots], axis=0)
        query_tile = queries[tile_row, tile_col].astype(jnp.float32).reshape(TILE, H, HEAD)
        key_heads = all_keys.reshape(-1, H, HEAD)
        val_heads = all_vals.reshape(-1, H, HEAD)
        scores = jnp.einsum("qhd,khd->hqk", query_tile, key_heads) * score_scale
        scores = jnp.where(usable[None, None, :], scores, -jnp.inf)
        row_max = jnp.max(scores, axis=-1, keepdims=True)
        weights = jnp.exp(scores - row_max)
        totals = jnp.sum(weights, axis=-1)
        rounded = lax.optimization_barrier(weights.astype(jnp.bfloat16)).astype(jnp.float32)
        mixed = jnp.einsum("hqk,khd->qhd", rounded, val_heads)
        mixed = mixed / jnp.transpose(totals)[:, :, None]
        return mixed.astype(jnp.bfloat16).reshape(TILE, HD)

    result = lax.map(one_tile, jnp.arange(tiles_h * tiles_w, dtype=jnp.int32))
    return result.reshape(tiles_h, tiles_w, TILE, HD)
```

```python
import functools
import math

import jax
import jax.numpy as jnp
from jax import lax
from jax.experimental import pallas as pl
from jax.experimental.pallas import tpu as pltpu
from jax.sharding import PartitionSpec as P

HEAD = 128
CUBE = 32
LOG_SCALE = HEAD ** -0.5 * math.log2(math.e)
NEG = -1e30
VMEM = 56 << 20


def dot_t(a, b):
    return lax.dot_general(a, b, (((1,), (1,)), ((), ())), preferred_element_type=jnp.float32)


def dot(a, b):
    return lax.dot_general(a, b, (((1,), (0,)), ((), ())), preferred_element_type=jnp.float32)


def partial_softmax(scores, vals):
    top = functools.reduce(jnp.maximum, [jnp.max(s, axis=1, keepdims=True) for s in scores])
    total = 0.0
    mixed = 0.0
    for s, v in zip(scores, vals):
        w = jnp.exp2((s - top) * LOG_SCALE)
        total = total + jnp.sum(w, axis=1, keepdims=True)
        mixed = mixed + dot(w.astype(jnp.bfloat16), v)
    return mixed / total, top * LOG_SCALE + jnp.log2(total)


def window_kernel(place, q, qu, qd, kl, kc, kr, vl, vc, vr, o, ou, od, lo, lu, ld):
    head = pl.program_id(0)
    lane = lax.broadcasted_iota(jnp.int32, (q.shape[1], HEAD), 1)
    keys = (kl, kc, kr)
    vals = (vl, vc, vr)

    def run(cols):
        for query, out, lse, rows in (
            (qu, ou, lu, (0,)),
            (qd, od, ld, (1,)),
            (q.at[0], o.at[0], lo.at[0], (0, 1)),
            (q.at[1], o.at[1], lo.at[1], (0, 1)),
        ):
            picks = [(c, r) for c in cols for r in rows]
            scores = [dot_t(query[...], keys[c][r]) for c, r in picks]
            mixed, level = partial_softmax(scores, [vals[c][r] for c, r in picks])
            out[...] = mixed.astype(out.dtype)
            lse[...] = jnp.where(lane == head, level, lse[...])

    first = place[0] == 0
    last = place[0] == place[1] - 1

    @pl.when(jnp.logical_not(first | last))
    def _():
        run((0, 1, 2))

    @pl.when(first)
    def _():
        run((1, 2))

    @pl.when(last)
    def _():
        run((0, 1))


def window(place, q, qu, qd, kl, kc, kr, vl, vc, vr):
    rows, tile, feat = q.shape
    heads = feat // HEAD
    two = pl.BlockSpec((rows, tile, HEAD), lambda h, *_: (0, 0, h))
    one = pl.BlockSpec((tile, HEAD), lambda h, *_: (0, h))
    two_c = pl.BlockSpec((rows, tile, HEAD), lambda h, *_: (0, 0, 0))
    one_c = pl.BlockSpec((tile, HEAD), lambda h, *_: (0, 0))
    f32 = jnp.float32
    shape = jax.ShapeDtypeStruct
    return pl.pallas_call(
        window_kernel,
        grid_spec=pltpu.PrefetchScalarGridSpec(
            num_scalar_prefetch=1,
            grid=(heads,),
            in_specs=[two, one, one] + [two] * 6,
            out_specs=[two, one, one, two_c, one_c, one_c],
        ),
        out_shape=[
            shape((rows, tile, feat), f32),
            shape((tile, feat), jnp.bfloat16),
            shape((tile, feat), jnp.bfloat16),
            shape((rows, tile, HEAD), f32),
            shape((tile, HEAD), f32),
            shape((tile, HEAD), f32),
        ],
        compiler_params=pltpu.CompilerParams(vmem_limit_bytes=VMEM),
        cost_estimate=pl.CostEstimate(
            flops=4 * rows * tile * 9 * tile * feat, bytes_accessed=30 << 20, transcendentals=rows * tile * 9 * tile * heads
        ),
        name="window",
    )(place, q, qu, qd, kl, kc, kr, vl, vc, vr)


def cube_kernel(spots, counts, has, q, ck, cv, o, lo, ou, od, lu, ld, out, kbuf, vbuf):
    head = pl.program_id(0)
    tile = q.shape[1]
    slots = spots.shape[1]
    lane = lax.broadcasted_iota(jnp.int32, (tile, HEAD), 1)

    def column(x):
        return jnp.sum(jnp.where(lane == head, x, 0.0), axis=1, keepdims=True)

    for t, (ext, lext) in enumerate(((od, ld), (ou, lu))):
        for s in range(slots):
            spot = spots[t, s]
            kbuf[t, s * CUBE : (s + 1) * CUBE, :] = ck[spot // 2, spot % 2]
            vbuf[t, s * CUBE : (s + 1) * CUBE, :] = cv[spot // 2, spot % 2]
        slot = lax.broadcasted_iota(jnp.int32, (1, slots * CUBE), 1) // CUBE
        scores = jnp.where(slot < counts[t], dot_t(q[t], kbuf[t]), NEG)
        mixed, level = partial_softmax([scores], [vbuf[t]])
        win_level = column(lo[t])
        ext_level = jnp.where(has[t] > 0, column(lext[...]), NEG)
        top = jnp.maximum(jnp.maximum(level, win_level), ext_level)
        a = jnp.exp2(level - top)
        b = jnp.exp2(win_level - top)
        c = jnp.exp2(ext_level - top)
        total = a + b + c
        out[t] = ((mixed * a + o[t] * b + ext[...].astype(jnp.float32) * c) / total).astype(out.dtype)


def cubes(spots, counts, has, q, fetched, o, lo, ou, od, lu, ld):
    rows, tile, feat = q.shape
    heads = feat // HEAD
    cols = fetched.shape[0]
    slots = spots.shape[1]
    two = pl.BlockSpec((rows, tile, HEAD), lambda h, *_: (0, 0, h))
    one = pl.BlockSpec((tile, HEAD), lambda h, *_: (0, h))
    two_c = pl.BlockSpec((rows, tile, HEAD), lambda h, *_: (0, 0, 0))
    one_c = pl.BlockSpec((tile, HEAD), lambda h, *_: (0, 0))
    ck = pl.BlockSpec((cols, None, 2, CUBE, HEAD), lambda h, *_: (0, 0, 0, 0, h))
    cv = pl.BlockSpec((cols, None, 2, CUBE, HEAD), lambda h, *_: (0, 1, 0, 0, h))
    return pl.pallas_call(
        cube_kernel,
        grid_spec=pltpu.PrefetchScalarGridSpec(
            num_scalar_prefetch=3,
            grid=(heads,),
            in_specs=[two, ck, cv, two, two_c, one, one, one_c, one_c],
            out_specs=two,
            scratch_shapes=[pltpu.VMEM((rows, slots * CUBE, HEAD), jnp.bfloat16)] * 2,
        ),
        out_shape=jax.ShapeDtypeStruct((rows, tile, feat), jnp.bfloat16),
        compiler_params=pltpu.CompilerParams(vmem_limit_bytes=VMEM),
        cost_estimate=pl.CostEstimate(
            flops=4 * rows * tile * slots * CUBE * feat, bytes_accessed=20 << 20, transcendentals=rows * tile * slots * CUBE * heads
        ),
        name="cubes",
    )(spots, counts, has, q, fetched, fetched, o, lo, ou, od, lu, ld)


def body(queries, keys, values, selected, counts):
    rows = queries.shape[0]
    tile = queries.shape[2]
    feat = queries.shape[3]
    slots = selected.shape[2]
    columns = lax.axis_size("wa")
    bands = lax.axis_size("ha")
    cubes_dev = rows * (tile // CUBE)
    q, k, v = (x[:, 0] for x in (queries, keys, values))
    right = [(i, i + 1) for i in range(columns - 1)]
    left = [(i + 1, i) for i in range(columns - 1)]
    down = [(i, i + 1) for i in range(bands - 1)]
    up = [(i + 1, i) for i in range(bands - 1)]

    kl, kr = lax.ppermute(k, "wa", right), lax.ppermute(k, "wa", left)
    vl, vr = lax.ppermute(v, "wa", right), lax.ppermute(v, "wa", left)
    qu, qd = lax.ppermute(q[1], "ha", down), lax.ppermute(q[0], "ha", up)

    ids = selected.reshape(rows * slots)
    owner = ids // cubes_dev
    local = ids % cubes_dev
    same = owner[:, None] == owner[None, :]
    before = jnp.arange(rows * slots)[:, None] > jnp.arange(rows * slots)[None, :]
    rank = jnp.sum((same & before).astype(jnp.int32), axis=1)
    spots = owner * 2 + rank
    place_at = spots[:, None] == jnp.arange(columns * 2, dtype=jnp.int32)[None, :]
    requests = jnp.sum(jnp.where(place_at, local[:, None], 0), axis=0).reshape(columns, 2)
    asked = lax.all_to_all(requests, "wa", split_axis=0, concat_axis=0, tiled=True)
    ktab = k.reshape(cubes_dev, CUBE, feat)
    vtab = v.reshape(cubes_dev, CUBE, feat)
    found = jnp.stack([ktab[asked], vtab[asked]], axis=1)
    fetched = lax.all_to_all(found, "wa", split_axis=0, concat_axis=0, tiled=True)

    row = lax.axis_index("ha")
    col = lax.axis_index("wa")
    place = jnp.stack([col, jnp.int32(columns)]).astype(jnp.int32)
    has = jnp.stack([row > 0, row < bands - 1]).astype(jnp.int32)
    o, ou, od, lo, lu, ld = window(place, q, qu, qd, kl, k, kr, vl, v, vr)
    ou, lu = lax.ppermute(ou, "ha", up), lax.ppermute(lu, "ha", up)
    od, ld = lax.ppermute(od, "ha", down), lax.ppermute(ld, "ha", down)
    out = cubes(spots.reshape(rows, slots), counts[:, 0], has, q, fetched, o, lo, ou, od, lu, ld)
    return out[:, None]


def solution(mesh):
    return jax.shard_map(
        body,
        mesh=mesh,
        in_specs=(
            P("ha", "wa", None, None),
            P("ha", "wa", None, None),
            P("ha", "wa", None, None),
            P("ha", "wa", None),
            P("ha", "wa"),
        ),
        out_specs=P("ha", "wa", None, None),
        check_vma=False,
    )
```

```python
import functools
import math

import jax
import jax.numpy as jnp
from jax import lax
from jax.experimental import pallas as pl
from jax.experimental.pallas import tpu as pltpu
from jax.sharding import PartitionSpec as P

HEAD = 128
CUBE = 32
DEPTH = 4
LOG_SCALE = HEAD ** -0.5 * math.log2(math.e)
NEG = -1e30
VMEM = 56 << 20


def dot_t(a, b):
    return lax.dot_general(a, b, (((1,), (1,)), ((), ())), preferred_element_type=jnp.float32)


def dot(a, b):
    return lax.dot_general(a, b, (((1,), (0,)), ((), ())), preferred_element_type=jnp.float32)


def partial_softmax(scores, vals):
    top = functools.reduce(jnp.maximum, [jnp.max(s, axis=1, keepdims=True) for s in scores])
    total = 0.0
    mixed = 0.0
    for s, v in zip(scores, vals):
        w = jnp.exp2((s - top) * LOG_SCALE)
        total = total + jnp.sum(w, axis=1, keepdims=True)
        mixed = mixed + dot(w.astype(jnp.bfloat16), v)
    return mixed / total, top * LOG_SCALE + jnp.log2(total)


def window_kernel(place, q, qu, qd, kl, kc, kr, vl, vc, vr, o, ou, od, lo, lu, ld):
    head = pl.program_id(0)
    lane = lax.broadcasted_iota(jnp.int32, (q.shape[1], HEAD), 1)
    keys = (kl, kc, kr)
    vals = (vl, vc, vr)

    def run(cols):
        for query, out, lse, rows in (
            (qu, ou, lu, (0,)),
            (qd, od, ld, (1,)),
            (q.at[0], o.at[0], lo.at[0], (0, 1)),
            (q.at[1], o.at[1], lo.at[1], (0, 1)),
        ):
            picks = [(c, r) for c in cols for r in rows]
            scores = [dot_t(query[...], keys[c][r]) for c, r in picks]
            mixed, level = partial_softmax(scores, [vals[c][r] for c, r in picks])
            out[...] = mixed.astype(out.dtype)
            lse[...] = jnp.where(lane == head, level, lse[...])

    first = place[0] == 0
    last = place[0] == place[1] - 1

    @pl.when(jnp.logical_not(first | last))
    def _():
        run((0, 1, 2))

    @pl.when(first)
    def _():
        run((1, 2))

    @pl.when(last)
    def _():
        run((0, 1))


def window(place, q, qu, qd, kl, kc, kr, vl, vc, vr):
    rows, tile, feat = q.shape
    heads = feat // HEAD
    two = pl.BlockSpec((rows, tile, HEAD), lambda h, *_: (0, 0, h))
    one = pl.BlockSpec((tile, HEAD), lambda h, *_: (0, h))
    two_c = pl.BlockSpec((rows, tile, HEAD), lambda h, *_: (0, 0, 0))
    one_c = pl.BlockSpec((tile, HEAD), lambda h, *_: (0, 0))
    f32 = jnp.float32
    shape = jax.ShapeDtypeStruct
    return pl.pallas_call(
        window_kernel,
        grid_spec=pltpu.PrefetchScalarGridSpec(
            num_scalar_prefetch=1,
            grid=(heads,),
            in_specs=[two, one, one] + [two] * 6,
            out_specs=[two, one, one, two_c, one_c, one_c],
        ),
        out_shape=[
            shape((rows, tile, feat), f32),
            shape((tile, feat), jnp.bfloat16),
            shape((tile, feat), jnp.bfloat16),
            shape((rows, tile, HEAD), f32),
            shape((tile, HEAD), f32),
            shape((tile, HEAD), f32),
        ],
        compiler_params=pltpu.CompilerParams(vmem_limit_bytes=VMEM),
        cost_estimate=pl.CostEstimate(
            flops=4 * rows * tile * 9 * tile * feat, bytes_accessed=30 << 20, transcendentals=rows * tile * 9 * tile * heads
        ),
        name="window",
    )(place, q, qu, qd, kl, kc, kr, vl, vc, vr)


def cube_kernel(slot_of, counts, has, q, *refs):
    sources, (o, lo, ou, od, lu, ld, out, kbuf, vbuf) = refs[:6], refs[6:]
    head = pl.program_id(0)
    rows, tile = q.shape[0], q.shape[1]
    lane = lax.broadcasted_iota(jnp.int32, (tile, HEAD), 1)

    def column(x):
        return jnp.sum(jnp.where(lane == head, x, 0.0), axis=1, keepdims=True)

    index = 0
    for ck, cv in (sources[0:2], sources[2:4], sources[4:6]):
        for at in range(ck.shape[0]):
            for rank in range(2):
                spot = pl.ds(pl.multiple_of(slot_of[index] * CUBE, CUBE), CUBE)
                kbuf[spot, :] = ck[at, rank]
                vbuf[spot, :] = cv[at, rank]
                index += 1
    span = index * CUBE // rows
    for t, (ext, lext) in enumerate(((od, ld), (ou, lu))):
        part = pl.ds(t * span, span)
        slot = lax.broadcasted_iota(jnp.int32, (1, span), 1) // CUBE
        scores = jnp.where(slot < counts[t], dot_t(q[t], kbuf[part, :]), NEG)
        mixed, level = partial_softmax([scores], [vbuf[part, :]])
        win_level = column(lo[t])
        ext_level = jnp.where(has[t] > 0, column(lext[...]), NEG)
        top = jnp.maximum(jnp.maximum(level, win_level), ext_level)
        a = jnp.exp2(level - top)
        b = jnp.exp2(win_level - top)
        c = jnp.exp2(ext_level - top)
        total = a + b + c
        out[t] = ((mixed * a + o[t] * b + ext[...].astype(jnp.float32) * c) / total).astype(out.dtype)


def cubes(slot_of, counts, has, q, own, near, far, o, lo, ou, od, lu, ld):
    rows, tile, feat = q.shape
    heads = feat // HEAD
    keys = slot_of.shape[0] * CUBE
    two = pl.BlockSpec((rows, tile, HEAD), lambda h, *_: (0, 0, h))
    one = pl.BlockSpec((tile, HEAD), lambda h, *_: (0, h))
    two_c = pl.BlockSpec((rows, tile, HEAD), lambda h, *_: (0, 0, 0))
    one_c = pl.BlockSpec((tile, HEAD), lambda h, *_: (0, 0))

    def block(x, kv):
        if x.ndim == 6:
            return pl.BlockSpec((x.shape[0], None, None, 2, CUBE, HEAD), lambda h, *_: (0, 0, kv, 0, 0, h))
        return pl.BlockSpec((x.shape[0], None, 2, CUBE, HEAD), lambda h, *_: (0, kv, 0, 0, h))

    near = near.reshape((-1,) + near.shape[2:])
    return pl.pallas_call(
        cube_kernel,
        grid_spec=pltpu.PrefetchScalarGridSpec(
            num_scalar_prefetch=3,
            grid=(heads,),
            in_specs=[two]
            + [block(x, kv) for x in (own, near, far) for kv in range(2)]
            + [two, two_c, one, one, one_c, one_c],
            out_specs=two,
            scratch_shapes=[pltpu.VMEM((keys, HEAD), jnp.bfloat16)] * 2,
        ),
        out_shape=jax.ShapeDtypeStruct((rows, tile, feat), jnp.bfloat16),
        compiler_params=pltpu.CompilerParams(vmem_limit_bytes=VMEM),
        cost_estimate=pl.CostEstimate(
            flops=4 * tile * keys * feat, bytes_accessed=20 << 20, transcendentals=tile * keys * heads
        ),
        name="cubes",
    )(slot_of, counts, has, q, own, own, near, near, far, far, o, lo, ou, od, lu, ld)


def pick_kernel(ids, *refs):
    tables, (out, held, into, back) = refs[:-4], refs[-4:]
    groups, sides, kinds, ranks = out.shape[:4]
    pairs = []
    for g in range(groups):
        for s in range(sides):
            for kv in range(kinds):
                table = tables[kv if len(tables) == kinds else s * kinds + kv]
                for r in range(ranks):
                    at = len(pairs)
                    pairs.append(
                        (
                            pltpu.make_async_copy(table.at[ids[g, s, r]], held.at[at], into.at[at]),
                            pltpu.make_async_copy(held.at[at], out.at[g, s, kv, r], back.at[at]),
                        )
                    )
    for read, _ in pairs:
        read.start()
    for read, write in pairs:
        read.wait()
        write.start()
    for _, write in pairs:
        write.wait()


def pick(ids, tables, name, weight):
    feat = tables[0].shape[-1]
    shape = ids.shape[:2] + (2,) + ids.shape[2:] + (CUBE, feat)
    tables = [x.reshape(-1, CUBE, feat) for x in tables]
    return pl.pallas_call(
        pick_kernel,
        grid_spec=pltpu.PrefetchScalarGridSpec(
            num_scalar_prefetch=1,
            grid=(1,),
            in_specs=[pl.BlockSpec(memory_space=pl.ANY)] * len(tables),
            out_specs=pl.BlockSpec(memory_space=pl.ANY),
            scratch_shapes=[
                pltpu.VMEM((math.prod(shape[:4]), CUBE, feat), tables[0].dtype),
                pltpu.SemaphoreType.DMA((math.prod(shape[:4]),)),
                pltpu.SemaphoreType.DMA((math.prod(shape[:4]),)),
            ],
        ),
        out_shape=jax.ShapeDtypeStruct(shape, tables[0].dtype),
        compiler_params=pltpu.CompilerParams(vmem_limit_bytes=VMEM),
        cost_estimate=pl.CostEstimate(flops=0, bytes_accessed=weight * math.prod(shape), transcendentals=0),
        name=name,
    )(ids, *tables)


def body(queries, keys, values, selected, counts):
    rows = queries.shape[0]
    tile = queries.shape[2]
    feat = queries.shape[3]
    slots = selected.shape[2]
    columns = lax.axis_size("wa")
    bands = lax.axis_size("ha")
    cubes_dev = rows * (tile // CUBE)
    q, k, v = (x[:, 0] for x in (queries, keys, values))
    down = [(i, i + 1) for i in range(bands - 1)]
    up = [(i + 1, i) for i in range(bands - 1)]
    lines = columns // DEPTH
    planes = [[line * DEPTH + z for line in range(lines)] for z in range(DEPTH)]
    spin = [(i, i - i % DEPTH + (i + 1) % DEPTH) for i in range(columns)]
    spun = [(j, i) for i, j in spin]
    across = [(i, i - i % DEPTH + (i + 2) % DEPTH) for i in range(columns)]
    ends = [(i, i + DEPTH) for i in range(0, columns - DEPTH, DEPTH)]
    ends = ends + [(j + DEPTH - 1, i + DEPTH - 1) for i, j in ends]
    steps = [(i, i + 1) for i in range(DEPTH - 1, columns - 1, DEPTH)]
    steps = steps + [(j, i) for i, j in steps]
    col = lax.axis_index("wa")
    z = col % DEPTH

    qu, qd = lax.ppermute(q[1], "ha", down), lax.ppermute(q[0], "ha", up)
    kl, kr = lax.ppermute(k, "wa", spin), lax.ppermute(k, "wa", spun)
    vl, vr = lax.ppermute(v, "wa", spin), lax.ppermute(v, "wa", spun)

    ids = selected.reshape(rows * slots)
    owner = ids // cubes_dev
    local = ids % cubes_dev
    same = owner[:, None] == owner[None, :]
    before = jnp.arange(rows * slots)[:, None] > jnp.arange(rows * slots)[None, :]
    rank = jnp.sum((same & before).astype(jnp.int32), axis=1)
    place_at = (owner * 2 + rank)[:, None] == jnp.arange(columns * 2, dtype=jnp.int32)[None, :]
    wanted = jnp.sum(jnp.where(place_at, local[:, None], 0), axis=0).reshape(columns, 2)
    wanted = wanted.reshape(lines, DEPTH, 2)
    wanted = jnp.stack([jnp.roll(wanted, 1, axis=1), wanted, jnp.roll(wanted, -1, axis=1)], axis=2)
    wanted = wanted.reshape(columns, 3, 2)
    asked = lax.all_to_all(wanted, "wa", split_axis=0, concat_axis=0, tiled=True)
    asked = asked.reshape(lines, DEPTH, 3, 2)
    asked_same = lax.dynamic_index_in_dim(asked, z, 1, keepdims=False)
    asked_far = lax.dynamic_index_in_dim(asked, (z + 2) % DEPTH, 1, keepdims=False)
    own = pick(jnp.stack([asked_same[:, 1], asked_far[:, 1]], axis=1), [k, v], "pick_own", 4)
    own = lax.all_to_all(own, "wa", split_axis=0, concat_axis=0, tiled=True, axis_index_groups=planes)
    far = lax.ppermute(own[:, 1], "wa", across)
    kb = lax.ppermute(jnp.where(z == 0, kl, kr), "wa", ends)
    vb = lax.ppermute(v, "wa", steps)
    kl, kr, vl, vr, kb, vb, qu, qd = lax.optimization_barrier((kl, kr, vl, vr, kb, vb, qu, qd))
    near = pick(jnp.stack([asked_same[:, 0], asked_same[:, 2]], axis=1), [kl, vl, kr, vr], "pick_near", 4)
    near = lax.all_to_all(near, "wa", split_axis=0, concat_axis=0, tiled=True, axis_index_groups=planes)
    kl, vl = jnp.where(z == 0, kb, kl), jnp.where(z == 0, vb, vl)
    kr, vr = jnp.where(z == DEPTH - 1, kb, kr), jnp.where(z == DEPTH - 1, vb, vr)

    ahead = (owner - z) % DEPTH
    line = owner // DEPTH
    spot = jnp.where(
        ahead == 0,
        line * 2,
        jnp.where(ahead == 2, 6 * lines + line * 2, 2 * lines + line * 4 + jnp.where(ahead == 1, 2, 0)),
    )
    spot = spot + rank
    entry = jnp.arange(rows * slots, dtype=jnp.int32)
    slot_of = jnp.sum(jnp.where(spot[:, None] == entry[None, :], entry[:, None], 0), axis=0)

    row = lax.axis_index("ha")
    place = jnp.stack([col, jnp.int32(columns)]).astype(jnp.int32)
    has = jnp.stack([row > 0, row < bands - 1]).astype(jnp.int32)
    o, ou, od, lo, lu, ld = window(place, q, qu, qd, kl, k, kr, vl, v, vr)
    ou, lu = lax.ppermute(ou, "ha", up), lax.ppermute(lu, "ha", up)
    od, ld = lax.ppermute(od, "ha", down), lax.ppermute(ld, "ha", down)
    out = cubes(slot_of, counts[:, 0], has, q, own, near, far, o, lo, ou, od, lu, ld)
    return out[:, None]


def solution(mesh):
    return jax.shard_map(
        body,
        mesh=mesh,
        in_specs=(
            P("ha", "wa", None, None),
            P("ha", "wa", None, None),
            P("ha", "wa", None, None),
            P("ha", "wa", None),
            P("ha", "wa"),
        ),
        out_specs=P("ha", "wa", None, None),
        check_vma=False,
    )
```

```python
import functools
import math

import jax
import jax.numpy as jnp
from jax import lax
from jax.experimental import pallas as pl
from jax.experimental.pallas import tpu as pltpu
from jax.sharding import PartitionSpec as P

HEAD = 128
CUBE = 32
LOG_SCALE = HEAD ** -0.5 * math.log2(math.e)
NEG = -1e30
VMEM = 56 << 20


def dot_t(a, b):
    return lax.dot_general(a, b, (((1,), (1,)), ((), ())), preferred_element_type=jnp.float32)


def dot(a, b):
    return lax.dot_general(a, b, (((1,), (0,)), ((), ())), preferred_element_type=jnp.float32)


def partial_softmax(scores, vals):
    top = functools.reduce(jnp.maximum, [jnp.max(s, axis=1, keepdims=True) for s in scores])
    total = 0.0
    mixed = 0.0
    for s, v in zip(scores, vals):
        w = jnp.exp2((s - top) * LOG_SCALE)
        total = total + jnp.sum(w, axis=1, keepdims=True)
        mixed = mixed + dot(w.astype(jnp.bfloat16), v)
    return mixed / total, top * LOG_SCALE + jnp.log2(total)


def window_kernel(rows_of, place, *refs):
    count = len(rows_of)
    queries, keys, vals = refs[:count], refs[count : count + 3], refs[count + 3 : count + 6]
    outs, levels = refs[count + 6 : 2 * count + 6], refs[2 * count + 6 :]
    head = pl.program_id(0)
    lane = lax.broadcasted_iota(jnp.int32, queries[0].shape, 1)

    def run(cols):
        for query, out, lse, rows in zip(queries, outs, levels, rows_of):
            picks = [(c, r) for c in cols for r in rows]
            scores = [dot_t(query[...], keys[c][r]) for c, r in picks]
            mixed, level = partial_softmax(scores, [vals[c][r] for c, r in picks])
            out[...] = mixed.astype(out.dtype)
            lse[...] = jnp.where(lane == head, level, lse[...])

    first = place[0] == 0
    last = place[0] == place[1] - 1

    @pl.when(jnp.logical_not(first | last))
    def _():
        run((0, 1, 2))

    @pl.when(first)
    def _():
        run((1, 2))

    @pl.when(last)
    def _():
        run((0, 1))


def window(place, queries, rows_of, keys, vals, dtype, name):
    tile, feat = queries[0].shape
    heads = feat // HEAD
    count = len(queries)
    tiles = 3 * sum(len(rows) for rows in rows_of)
    two = pl.BlockSpec((keys[0].shape[0], tile, HEAD), lambda h, *_: (0, 0, h))
    one = pl.BlockSpec((tile, HEAD), lambda h, *_: (0, h))
    level = pl.BlockSpec((tile, HEAD), lambda h, *_: (0, 0))
    shape = jax.ShapeDtypeStruct
    out = pl.pallas_call(
        functools.partial(window_kernel, rows_of),
        grid_spec=pltpu.PrefetchScalarGridSpec(
            num_scalar_prefetch=1,
            grid=(heads,),
            in_specs=[one] * count + [two] * 6,
            out_specs=[one] * count + [level] * count,
        ),
        out_shape=[shape((tile, feat), dtype)] * count + [shape((tile, HEAD), jnp.float32)] * count,
        compiler_params=pltpu.CompilerParams(vmem_limit_bytes=VMEM),
        cost_estimate=pl.CostEstimate(
            flops=4 * tile * tiles * tile * feat, bytes_accessed=20 << 20, transcendentals=tile * tiles * tile * heads
        ),
        name=name,
    )(place, *queries, *keys, *vals)
    return out[:count], out[count:]


def cube_kernel(slot_of, counts, has, q, *refs):
    sources, (o0, o1, lo0, lo1, ou, od, lu, ld, out, kbuf, vbuf) = refs[:6], refs[6:]
    rows, tile, width = q.shape
    lane = lax.broadcasted_iota(jnp.int32, (tile, HEAD), 1)
    index = 0
    for ck, cv in (sources[0:2], sources[2:4], sources[4:6]):
        for at in range(ck.shape[0]):
            for rank in range(ck.shape[1]):
                spot = pl.ds(pl.multiple_of(slot_of[index] * CUBE, CUBE), CUBE)
                kbuf[spot, :] = ck[at, rank]
                vbuf[spot, :] = cv[at, rank]
                index += 1
    span = index * CUBE // rows
    half = span // 2
    slot = half // CUBE + lax.broadcasted_iota(jnp.int32, (1, half), 1) // CUBE
    for part in range(width // HEAD):
        lanes = slice(part * HEAD, (part + 1) * HEAD)
        head = pl.program_id(0) * (width // HEAD) + part

        def column(x):
            return jnp.sum(jnp.where(lane == head, x, 0.0), axis=1, keepdims=True)

        scores = []
        for t in range(rows):
            live = dot_t(q[t, :, lanes], kbuf[pl.ds(t * span, half), lanes])
            rest = dot_t(q[t, :, lanes], kbuf[pl.ds(t * span + half, half), lanes])
            scores.append((live, jnp.where(slot < counts[t], rest, NEG)))
        for t, (o, lo, ext, lext) in enumerate(((o0, lo0, od, ld), (o1, lo1, ou, lu))):
            vals = [vbuf[pl.ds(t * span + i * half, half), lanes] for i in range(2)]
            mixed, level = partial_softmax(scores[t], vals)
            win_level = column(lo[...])
            ext_level = jnp.where(has[t] > 0, column(lext[...]), NEG)
            top = jnp.maximum(jnp.maximum(level, win_level), ext_level)
            a = jnp.exp2(level - top)
            b = jnp.exp2(win_level - top)
            c = jnp.exp2(ext_level - top)
            norm = 1.0 / (a + b + c)
            mixed = mixed * (a * norm) + o[:, lanes] * (b * norm) + ext[:, lanes].astype(jnp.float32) * (c * norm)
            out[t, :, lanes] = mixed.astype(out.dtype)


def cubes(slot_of, counts, has, q, early, near, far, o, lo, ou, od, lu, ld):
    rows, tile, feat = q.shape
    heads = feat // HEAD
    width = 2 * HEAD
    keys = slot_of.shape[0] * CUBE
    two = pl.BlockSpec((rows, tile, width), lambda h, *_: (0, 0, h))
    one = pl.BlockSpec((tile, width), lambda h, *_: (0, h))
    one_c = pl.BlockSpec((tile, HEAD), lambda h, *_: (0, 0))

    def block(x, kv):
        return pl.BlockSpec((x.shape[0], None, 1, CUBE, width), lambda h, *_: (0, kv, 0, 0, h))

    mine = pl.BlockSpec((early.shape[0], None, None, 1, CUBE, width), lambda h, *_: (0, 2, 0, 0, 0, h))
    mine_v = pl.BlockSpec((early.shape[0], None, None, 1, CUBE, width), lambda h, *_: (0, 2, 1, 0, 0, h))
    near, far = (x.reshape((-1,) + x.shape[2:]) for x in (near, far))
    return pl.pallas_call(
        cube_kernel,
        grid_spec=pltpu.PrefetchScalarGridSpec(
            num_scalar_prefetch=3,
            grid=(feat // width,),
            in_specs=[two]
            + [mine, mine_v]
            + [block(x, kv) for x in (near, far) for kv in range(2)]
            + [one, one, one_c, one_c, one, one, one_c, one_c],
            out_specs=two,
            scratch_shapes=[pltpu.VMEM((keys, width), jnp.bfloat16)] * 2,
        ),
        out_shape=jax.ShapeDtypeStruct((rows, tile, feat), jnp.bfloat16),
        compiler_params=pltpu.CompilerParams(vmem_limit_bytes=VMEM),
        cost_estimate=pl.CostEstimate(
            flops=4 * tile * keys * feat, bytes_accessed=20 << 20, transcendentals=tile * keys * heads
        ),
        name="cubes",
    )(slot_of, counts, has, q, early, early, near, near, far, far, *o, *lo, ou, od, lu, ld)


def pick_kernel(ids, *refs):
    tables, (out, held, into, back) = refs[:-4], refs[-4:]
    groups, sides, kinds, ranks = out.shape[:4]
    pairs = []
    for g in range(groups):
        for s in range(sides):
            for kv in range(kinds):
                table = tables[kv if len(tables) == kinds else s * kinds + kv]
                for r in range(ranks):
                    at = len(pairs)
                    pairs.append(
                        (
                            pltpu.make_async_copy(table.at[ids[g, s, r]], held.at[at], into.at[at]),
                            pltpu.make_async_copy(held.at[at], out.at[g, s, kv, r], back.at[at]),
                        )
                    )
    for read, _ in pairs:
        read.start()
    for read, write in pairs:
        read.wait()
        write.start()
    for _, write in pairs:
        write.wait()


def pick(ids, tables, kinds, name):
    feat = tables[0].shape[-1]
    shape = ids.shape[:2] + (kinds,) + ids.shape[2:] + (CUBE, feat)
    tables = [x.reshape(-1, CUBE, feat) for x in tables]
    return pl.pallas_call(
        pick_kernel,
        grid_spec=pltpu.PrefetchScalarGridSpec(
            num_scalar_prefetch=1,
            grid=(1,),
            in_specs=[pl.BlockSpec(memory_space=pl.ANY)] * len(tables),
            out_specs=pl.BlockSpec(memory_space=pl.ANY),
            scratch_shapes=[
                pltpu.VMEM((math.prod(shape[:4]), CUBE, feat), tables[0].dtype),
                pltpu.SemaphoreType.DMA((math.prod(shape[:4]),)),
                pltpu.SemaphoreType.DMA((math.prod(shape[:4]),)),
            ],
        ),
        out_shape=jax.ShapeDtypeStruct(shape, tables[0].dtype),
        compiler_params=pltpu.CompilerParams(vmem_limit_bytes=VMEM),
        cost_estimate=pl.CostEstimate(flops=0, bytes_accessed=4 * math.prod(shape), transcendentals=0),
        name=name,
    )(ids, *tables)


DEPTH = 4


def body(queries, keys, values, selected, counts):
    rows = queries.shape[0]
    tile = queries.shape[2]
    feat = queries.shape[3]
    slots = selected.shape[2]
    columns = lax.axis_size("wa")
    bands = lax.axis_size("ha")
    cubes_dev = rows * (tile // CUBE)
    q, k, v = (x[:, 0] for x in (queries, keys, values))
    down = [(i, i + 1) for i in range(bands - 1)]
    up = [(i + 1, i) for i in range(bands - 1)]
    lines = columns // DEPTH
    planes = [[line * DEPTH + z for line in range(lines)] for z in range(DEPTH)]
    right = [(i, (i + 1) % columns) for i in range(columns)]
    left = [(j, i) for i, j in right]
    spin = [(i, i - i % DEPTH + (i + 1) % DEPTH) for i in range(columns)]
    spun = [(j, i) for i, j in spin]
    across = [(i, i - i % DEPTH + (i + 2) % DEPTH) for i in range(columns)]
    onto = [(i, (i + DEPTH) % columns) for i in range(0, columns, DEPTH)]
    onto = onto + [(j + DEPTH - 1, i + DEPTH - 1) for i, j in onto]
    col = lax.axis_index("wa")
    z = col % DEPTH

    ids = selected.reshape(rows * slots)
    owner = ids // cubes_dev
    local = ids % cubes_dev
    same = owner[:, None] == owner[None, :]
    before = jnp.arange(rows * slots)[:, None] > jnp.arange(rows * slots)[None, :]
    rank = jnp.sum((same & before).astype(jnp.int32), axis=1)
    place_at = (owner * 2 + rank)[:, None] == jnp.arange(columns * 2, dtype=jnp.int32)[None, :]
    wanted = jnp.sum(jnp.where(place_at, local[:, None], 0), axis=0).reshape(columns, 2)
    wanted = jnp.stack([jnp.roll(wanted, 1, axis=0), wanted, jnp.roll(wanted, -1, axis=0)], axis=1)
    asked = lax.all_to_all(wanted, "wa", split_axis=0, concat_axis=0, tiled=True)
    q_next, v_next, asked = lax.optimization_barrier((q, v, asked))
    qu, qd = lax.ppermute(q_next[1], "ha", down), lax.ppermute(q_next[0], "ha", up)
    vl, vr = lax.ppermute(v_next, "wa", spin), lax.ppermute(v_next, "wa", spun)
    asked = asked.reshape(lines, DEPTH, 3, 2)
    asked_same = lax.dynamic_index_in_dim(asked, z, 1, keepdims=False)
    asked_far = lax.dynamic_index_in_dim(asked, (z + 2) % DEPTH, 1, keepdims=False)
    early = jnp.stack([asked_far[:, 1, 0], asked_far[:, 1, 1], asked_same[:, 1, 0]], axis=1)
    early = pick(early[:, :, None], [k, v] * 3, 2, "pick_early")
    early = lax.all_to_all(early, "wa", split_axis=0, concat_axis=0, tiled=True, axis_index_groups=planes)
    wrap, early = lax.optimization_barrier((jnp.where(z == 0, vl, vr), early))
    vb = lax.ppermute(wrap, "wa", onto)
    k_next, _, _ = lax.optimization_barrier((k, vl, vr))
    kl, kr = lax.ppermute(k_next, "wa", right), lax.ppermute(k_next, "wa", left)
    vl, vr = jnp.where(z == 0, vb, vl), jnp.where(z == DEPTH - 1, vb, vr)
    far = lax.ppermute(early[:, :2], "wa", across)
    kl, kr, vl, vr, qu, qd = lax.optimization_barrier((kl, kr, vl, vr, qu, qd))
    late = jnp.concatenate([asked_same[:, 0], asked_same[:, 1, 1:], asked_same[:, 2]], axis=1)
    near = pick(late[:, :, None], [kl, vl, kl, vl, k, v, kr, vr, kr, vr], 2, "pick_near")
    near = lax.all_to_all(near, "wa", split_axis=0, concat_axis=0, tiled=True, axis_index_groups=planes)

    ahead = (owner - z) % DEPTH
    line = ((owner - jnp.where(ahead == 1, 1, 0) + jnp.where(ahead == 3, 1, 0)) % columns) // DEPTH
    near_at = jnp.where(ahead == 0, 2, jnp.where(ahead == 1, 3 + rank, rank))
    spot = jnp.where(
        ahead == 2, 6 * lines + line * 2 + rank, jnp.where((ahead == 0) & (rank == 0), line, lines + line * 5 + near_at)
    )
    entry = jnp.arange(rows * slots, dtype=jnp.int32)
    slot_of = jnp.sum(jnp.where(spot[:, None] == entry[None, :], entry[:, None], 0), axis=0)

    row = lax.axis_index("ha")
    place = jnp.stack([col, jnp.int32(columns)]).astype(jnp.int32)
    has = jnp.stack([row > 0, row < bands - 1]).astype(jnp.int32)
    near_keys, near_vals = (kl, k, kr), (vl, v, vr)
    edge, edge_level = window(place, (qu, qd), ((0,), (1,)), near_keys, near_vals, jnp.bfloat16, "window_edge")
    ou, lu = lax.ppermute(edge[0], "ha", up), lax.ppermute(edge_level[0], "ha", up)
    od, ld = lax.ppermute(edge[1], "ha", down), lax.ppermute(edge_level[1], "ha", down)
    o, lo = window(place, (q[0], q[1]), ((0, 1), (0, 1)), near_keys, near_vals, jnp.float32, "window_own")
    out = cubes(slot_of, counts[:, 0], has, q, early, near, far, o, lo, ou, od, lu, ld)
    return out[:, None]


def solution(mesh):
    return jax.shard_map(
        body,
        mesh=mesh,
        in_specs=(
            P("ha", "wa", None, None),
            P("ha", "wa", None, None),
            P("ha", "wa", None, None),
            P("ha", "wa", None),
            P("ha", "wa"),
        ),
        out_specs=P("ha", "wa", None, None),
        check_vma=False,
    )
```

```python
import functools
import math

import jax
import jax.numpy as jnp
from jax import lax
from jax.experimental import pallas as pl
from jax.experimental.pallas import tpu as pltpu
from jax.sharding import PartitionSpec as P

HEAD = 128
CUBE = 32
LOG_SCALE = HEAD ** -0.5 * math.log2(math.e)
NEG = -1e30
VMEM = 56 << 20


def dot_t(a, b):
    return lax.dot_general(a, b, (((1,), (1,)), ((), ())), preferred_element_type=jnp.float32)


def dot(a, b):
    return lax.dot_general(a, b, (((1,), (0,)), ((), ())), preferred_element_type=jnp.float32)


def partial_softmax(scores, vals):
    top = functools.reduce(jnp.maximum, [jnp.max(s, axis=1, keepdims=True) for s in scores])
    total = 0.0
    mixed = 0.0
    shift = top * LOG_SCALE
    for s, v in zip(scores, vals):
        w = jnp.exp2(s * LOG_SCALE - shift)
        total = total + jnp.sum(w, axis=1, keepdims=True)
        mixed = mixed + dot(w.astype(jnp.bfloat16), v)
    return mixed / total, shift + jnp.log2(total)


def window_kernel(rows_of, place, *refs):
    count = len(rows_of)
    queries, keys, vals = refs[:count], refs[count : count + 3], refs[count + 3 : count + 6]
    outs, levels = refs[count + 6 : 2 * count + 6], refs[2 * count + 6 :]
    head = pl.program_id(0)
    lane = lax.broadcasted_iota(jnp.int32, queries[0].shape, 1)

    def run(cols):
        for query, out, lse, rows in zip(queries, outs, levels, rows_of):
            picks = [(c, r) for c in cols for r in rows]
            scores = [dot_t(query[...], keys[c][r]) for c, r in picks]
            mixed, level = partial_softmax(scores, [vals[c][r] for c, r in picks])
            out[...] = mixed.astype(out.dtype)
            lse[...] = jnp.where(lane == head, level, lse[...])

    first = place[0] == 0
    last = place[0] == place[1] - 1

    @pl.when(jnp.logical_not(first | last))
    def _():
        run((0, 1, 2))

    @pl.when(first)
    def _():
        run((1, 2))

    @pl.when(last)
    def _():
        run((0, 1))


def window(place, queries, rows_of, keys, vals, dtype, name):
    tile, feat = queries[0].shape
    heads = feat // HEAD
    count = len(queries)
    tiles = 3 * sum(len(rows) for rows in rows_of)
    two = pl.BlockSpec((keys[0].shape[0], tile, HEAD), lambda h, *_: (0, 0, h))
    one = pl.BlockSpec((tile, HEAD), lambda h, *_: (0, h))
    level = pl.BlockSpec((tile, HEAD), lambda h, *_: (0, 0))
    shape = jax.ShapeDtypeStruct
    out = pl.pallas_call(
        functools.partial(window_kernel, rows_of),
        grid_spec=pltpu.PrefetchScalarGridSpec(
            num_scalar_prefetch=1,
            grid=(heads,),
            in_specs=[one] * count + [two] * 6,
            out_specs=[one] * count + [level] * count,
        ),
        out_shape=[shape((tile, feat), dtype)] * count + [shape((tile, HEAD), jnp.float32)] * count,
        compiler_params=pltpu.CompilerParams(vmem_limit_bytes=VMEM),
        cost_estimate=pl.CostEstimate(
            flops=4 * tile * tiles * tile * feat, bytes_accessed=20 << 20, transcendentals=tile * tiles * tile * heads
        ),
        name=name,
    )(place, *queries, *keys, *vals)
    return out[:count], out[count:]


def cube_kernel(slot_of, counts, has, q, *refs):
    sources, (o0, o1, lo0, lo1, ou, od, lu, ld, out, kbuf, vbuf) = refs[:6], refs[6:]
    rows, tile, width = q.shape
    lane = lax.broadcasted_iota(jnp.int32, (tile, HEAD), 1)
    index = 0
    for ck, cv in (sources[0:2], sources[2:4], sources[4:6]):
        for at in range(ck.shape[0]):
            for rank in range(ck.shape[1]):
                spot = pl.ds(pl.multiple_of(slot_of[index] * CUBE, CUBE), CUBE)
                kbuf[spot, :] = ck[at, rank]
                vbuf[spot, :] = cv[at, rank]
                index += 1
    span = index * CUBE // rows
    half = span // 2
    slot = half // CUBE + lax.broadcasted_iota(jnp.int32, (1, half), 1) // CUBE
    for part in range(width // HEAD):
        lanes = slice(part * HEAD, (part + 1) * HEAD)
        head = pl.program_id(0) * (width // HEAD) + part

        def column(x):
            return jnp.sum(jnp.where(lane == head, x, 0.0), axis=1, keepdims=True)

        scores = []
        for t in range(rows):
            live = dot_t(q[t, :, lanes], kbuf[pl.ds(t * span, half), lanes])
            rest = dot_t(q[t, :, lanes], kbuf[pl.ds(t * span + half, half), lanes])
            scores.append((live, jnp.where(slot < counts[t], rest, NEG)))
        for t, (o, lo, ext, lext) in enumerate(((o0, lo0, od, ld), (o1, lo1, ou, lu))):
            vals = [vbuf[pl.ds(t * span + i * half, half), lanes] for i in range(2)]
            mixed, level = partial_softmax(scores[t], vals)
            win_level = column(lo[...])
            ext_level = jnp.where(has[t] > 0, column(lext[...]), NEG)
            top = jnp.maximum(jnp.maximum(level, win_level), ext_level)
            a = jnp.exp2(level - top)
            b = jnp.exp2(win_level - top)
            c = jnp.exp2(ext_level - top)
            norm = 1.0 / (a + b + c)
            mixed = mixed * (a * norm) + o[:, lanes] * (b * norm) + ext[:, lanes].astype(jnp.float32) * (c * norm)
            out[t, :, lanes] = mixed.astype(out.dtype)


def cubes(slot_of, counts, has, q, early, near, far, o, lo, ou, od, lu, ld):
    rows, tile, feat = q.shape
    heads = feat // HEAD
    width = 2 * HEAD
    keys = slot_of.shape[0] * CUBE
    two = pl.BlockSpec((rows, tile, width), lambda h, *_: (0, 0, h))
    one = pl.BlockSpec((tile, width), lambda h, *_: (0, h))
    one_c = pl.BlockSpec((tile, HEAD), lambda h, *_: (0, 0))

    def block(x, kv):
        return pl.BlockSpec((x.shape[0], None, 1, CUBE, width), lambda h, *_: (0, kv, 0, 0, h))

    mine = pl.BlockSpec((early.shape[0], None, None, 1, CUBE, width), lambda h, *_: (0, 2, 0, 0, 0, h))
    mine_v = pl.BlockSpec((early.shape[0], None, None, 1, CUBE, width), lambda h, *_: (0, 2, 1, 0, 0, h))
    near, far = (x.reshape((-1,) + x.shape[2:]) for x in (near, far))
    return pl.pallas_call(
        cube_kernel,
        grid_spec=pltpu.PrefetchScalarGridSpec(
            num_scalar_prefetch=3,
            grid=(feat // width,),
            in_specs=[two]
            + [mine, mine_v]
            + [block(x, kv) for x in (near, far) for kv in range(2)]
            + [one, one, one_c, one_c, one, one, one_c, one_c],
            out_specs=two,
            scratch_shapes=[pltpu.VMEM((keys, width), jnp.bfloat16)] * 2,
        ),
        out_shape=jax.ShapeDtypeStruct((rows, tile, feat), jnp.bfloat16),
        compiler_params=pltpu.CompilerParams(vmem_limit_bytes=VMEM),
        cost_estimate=pl.CostEstimate(
            flops=4 * tile * keys * feat, bytes_accessed=20 << 20, transcendentals=tile * keys * heads
        ),
        name="cubes",
    )(slot_of, counts, has, q, early, early, near, near, far, far, *o, *lo, ou, od, lu, ld)


def pick_kernel(ids, *refs):
    tables, (out, held, into, back) = refs[:-4], refs[-4:]
    groups, sides, kinds, ranks = out.shape[:4]
    pairs = []
    for g in range(groups):
        for s in range(sides):
            for kv in range(kinds):
                table = tables[kv if len(tables) == kinds else s * kinds + kv]
                for r in range(ranks):
                    at = len(pairs)
                    pairs.append(
                        (
                            pltpu.make_async_copy(table.at[ids[g, s, r]], held.at[at], into.at[at]),
                            pltpu.make_async_copy(held.at[at], out.at[g, s, kv, r], back.at[at]),
                        )
                    )
    for read, _ in pairs:
        read.start()
    for read, write in pairs:
        read.wait()
        write.start()
    for _, write in pairs:
        write.wait()


def pick(ids, tables, kinds, name):
    feat = tables[0].shape[-1]
    shape = ids.shape[:2] + (kinds,) + ids.shape[2:] + (CUBE, feat)
    tables = [x.reshape(-1, CUBE, feat) for x in tables]
    return pl.pallas_call(
        pick_kernel,
        grid_spec=pltpu.PrefetchScalarGridSpec(
            num_scalar_prefetch=1,
            grid=(1,),
            in_specs=[pl.BlockSpec(memory_space=pl.ANY)] * len(tables),
            out_specs=pl.BlockSpec(memory_space=pl.ANY),
            scratch_shapes=[
                pltpu.VMEM((math.prod(shape[:4]), CUBE, feat), tables[0].dtype),
                pltpu.SemaphoreType.DMA((math.prod(shape[:4]),)),
                pltpu.SemaphoreType.DMA((math.prod(shape[:4]),)),
            ],
        ),
        out_shape=jax.ShapeDtypeStruct(shape, tables[0].dtype),
        compiler_params=pltpu.CompilerParams(vmem_limit_bytes=VMEM),
        cost_estimate=pl.CostEstimate(flops=0, bytes_accessed=4 * math.prod(shape), transcendentals=0),
        name=name,
    )(ids, *tables)


DEPTH = 4


def body(queries, keys, values, selected, counts):
    rows = queries.shape[0]
    tile = queries.shape[2]
    feat = queries.shape[3]
    slots = selected.shape[2]
    columns = lax.axis_size("wa")
    bands = lax.axis_size("ha")
    cubes_dev = rows * (tile // CUBE)
    q, k, v = (x[:, 0] for x in (queries, keys, values))
    down = [(i, i + 1) for i in range(bands - 1)]
    up = [(i + 1, i) for i in range(bands - 1)]
    lines = columns // DEPTH
    planes = [[line * DEPTH + z for line in range(lines)] for z in range(DEPTH)]
    right = [(i, (i + 1) % columns) for i in range(columns)]
    left = [(j, i) for i, j in right]
    spin = [(i, i - i % DEPTH + (i + 1) % DEPTH) for i in range(columns)]
    spun = [(j, i) for i, j in spin]
    across = [(i, i - i % DEPTH + (i + 2) % DEPTH) for i in range(columns)]
    onto = [(i, (i + DEPTH) % columns) for i in range(0, columns, DEPTH)]
    onto = onto + [(j + DEPTH - 1, i + DEPTH - 1) for i, j in onto]
    col = lax.axis_index("wa")
    z = col % DEPTH

    ids = selected.reshape(rows * slots)
    owner = ids // cubes_dev
    local = ids % cubes_dev
    same = owner[:, None] == owner[None, :]
    before = jnp.arange(rows * slots)[:, None] > jnp.arange(rows * slots)[None, :]
    rank = jnp.sum((same & before).astype(jnp.int32), axis=1)
    place_at = (owner * 2 + rank)[:, None] == jnp.arange(columns * 2, dtype=jnp.int32)[None, :]
    wanted = jnp.sum(jnp.where(place_at, local[:, None], 0), axis=0).reshape(columns, 2)
    wanted = jnp.stack([jnp.roll(wanted, 1, axis=0), wanted, jnp.roll(wanted, -1, axis=0)], axis=1)
    asked = lax.all_to_all(wanted, "wa", split_axis=0, concat_axis=0, tiled=True)
    q_next, v_next, asked = lax.optimization_barrier((q, v, asked))
    qu, qd = lax.ppermute(q_next[1], "ha", down), lax.ppermute(q_next[0], "ha", up)
    vl, vr = lax.ppermute(v_next, "wa", spin), lax.ppermute(v_next, "wa", spun)
    asked = asked.reshape(lines, DEPTH, 3, 2)
    asked_same = lax.dynamic_index_in_dim(asked, z, 1, keepdims=False)
    asked_far = lax.dynamic_index_in_dim(asked, (z + 2) % DEPTH, 1, keepdims=False)
    early = jnp.stack([asked_far[:, 1, 0], asked_far[:, 1, 1], asked_same[:, 1, 0]], axis=1)
    early = pick(early[:, :, None], [k, v] * 3, 2, "pick_early")
    early = lax.all_to_all(early, "wa", split_axis=0, concat_axis=0, tiled=True, axis_index_groups=planes)
    wrap, early = lax.optimization_barrier((jnp.where(z == 0, vl, vr), early))
    vb = lax.ppermute(wrap, "wa", onto)
    k_next, _, _ = lax.optimization_barrier((k, vl, vr))
    kl, kr = lax.ppermute(k_next, "wa", right), lax.ppermute(k_next, "wa", left)
    vl, vr = jnp.where(z == 0, vb, vl), jnp.where(z == DEPTH - 1, vb, vr)
    far, kl, kr, vl, vr, qu, qd = lax.optimization_barrier((early[:, :2], kl, kr, vl, vr, qu, qd))
    far = lax.ppermute(far, "wa", across)
    late = jnp.concatenate([asked_same[:, 0], asked_same[:, 1, 1:], asked_same[:, 2]], axis=1)
    near = pick(late[:, :, None], [kl, vl, kl, vl, k, v, kr, vr, kr, vr], 2, "pick_near")
    near = lax.all_to_all(near, "wa", split_axis=0, concat_axis=0, tiled=True, axis_index_groups=planes)

    ahead = (owner - z) % DEPTH
    line = ((owner - jnp.where(ahead == 1, 1, 0) + jnp.where(ahead == 3, 1, 0)) % columns) // DEPTH
    near_at = jnp.where(ahead == 0, 2, jnp.where(ahead == 1, 3 + rank, rank))
    spot = jnp.where(
        ahead == 2, 6 * lines + line * 2 + rank, jnp.where((ahead == 0) & (rank == 0), line, lines + line * 5 + near_at)
    )
    entry = jnp.arange(rows * slots, dtype=jnp.int32)
    slot_of = jnp.sum(jnp.where(spot[:, None] == entry[None, :], entry[:, None], 0), axis=0)

    row = lax.axis_index("ha")
    place = jnp.stack([col, jnp.int32(columns)]).astype(jnp.int32)
    has = jnp.stack([row > 0, row < bands - 1]).astype(jnp.int32)
    near_keys, near_vals = (kl, k, kr), (vl, v, vr)
    edge, edge_level = window(place, (qu, qd), ((0,), (1,)), near_keys, near_vals, jnp.bfloat16, "window_edge")
    ou, lu = lax.ppermute(edge[0], "ha", up), lax.ppermute(edge_level[0], "ha", up)
    od, ld = lax.ppermute(edge[1], "ha", down), lax.ppermute(edge_level[1], "ha", down)
    o, lo = window(place, (q[0], q[1]), ((0, 1), (0, 1)), near_keys, near_vals, jnp.float32, "window_own")
    out = cubes(slot_of, counts[:, 0], has, q, early, near, far, o, lo, ou, od, lu, ld)
    return out[:, None]


def solution(mesh):
    return jax.shard_map(
        body,
        mesh=mesh,
        in_specs=(
            P("ha", "wa", None, None),
            P("ha", "wa", None, None),
            P("ha", "wa", None, None),
            P("ha", "wa", None),
            P("ha", "wa"),
        ),
        out_specs=P("ha", "wa", None, None),
        check_vma=False,
    )
```
